32 devices in a mesh: tok: 8 (over y, x, core), feat: 4 (over z).
Axes of the slice: x: 2, y: 2, z: 4, core: 2. Of those that a mesh axis runs over, the one named last changes fastest.
Arguments:
- resid: bfloat16 [1024, 4096], P('tok'), may hold values from -6 to 6
- enc_weight: bfloat16 [4096, 32768], P(None, ('tok', 'feat')), may hold values from -0.09375 to 0.09375
- enc_bias: float32 [32768], P(('tok', 'feat')), may hold values from -3 to 3
- dec_weight: bfloat16 [32768, 4096], P(('tok', 'feat')), may hold values from -0.0546875 to 0.0546875
- dec_bias: float32 [4096], replicated, may hold values from -3 to 3
- active_ids: int32 [8, 96], replicated, may hold values from 0 to 255, all different within a row; in each aligned block of 8 rows (0 to 7, 8 to 15, ...) at most 4 rows name the same one
Outputs:
- recon_error: float32 [1024, 4096], P('tok', 'feat')
The draws below stay inside these ranges and needn't reach their ends.
Inputs may be any that keep to these rules, and one draw needn't show every extreme that they name: `active_ids`: the ids of one row block are distinct; each feature block is active in at least one and at most 4 row blocks, and some feature block in exactly 4.
All inputs are finite; a program needn't handle non-finite values.
Results may differ from the reference program's by a relative error of at most 0.009.
Values may be sent and summed in bfloat16 or wider, within the bound.
A program may use at most 192 MiB of HBM per device.

```python
import math
import jax
import jax.numpy as jnp
import numpy as np
from jax import lax

D = 4096
BLK = 128
BLK_DEV = 8
ACT = 96
ROWS = 1024
RB = 8
NBLK = 256
MOST = 4
F = 32768
N_TOK = 8
N_FEAT = 4


def shard_levels(stream_key, dims, cuts, low, top_value):
    factor_of = 1.0
    for dim, blocks in cuts:
        draws = jax.random.uniform(jax.random.fold_in(jax.random.fold_in(stream_key, 6), dim), (blocks,), jnp.float32, low / len(cuts), top_value / len(cuts))
        factor_of = factor_of * jnp.repeat(jnp.exp(draws), dims[dim] // blocks).reshape((-1,) + (1,) * (len(dims) - 1 - dim))
    return factor_of


def shared_out(stream_key, own, number, rows, amount, top, bound, slope):
    order = jax.random.permutation(stream_key, amount)
    crowded, ordinary = shares(amount, rows * top, bound, slope, True), shares(amount, rows * top, bound, slope, False)
    places = jnp.arange(amount)

    def named(lengths, turn):
        used = int((lengths > 0).sum())
        fixed = max(1, used // 4)
        moved = fixed + (places - fixed + turn * (used - fixed)) % max(1, amount - fixed)
        return jnp.zeros((amount,), jnp.int32).at[order[jnp.where(places < fixed, places, moved)]].set(jnp.asarray(lengths, jnp.int32))

    lengths = jnp.where(number % 4 == 0, named(crowded, number // 4), named(ordinary, number - number // 4 - 1))
    mixed = jax.random.permutation(jax.random.fold_in(own, 3), amount)
    donor, receiver = mixed[0:amount // 2 * 2:2], mixed[1:amount // 2 * 2:2]
    room = jnp.minimum(lengths[donor] - 1, bound - lengths[receiver]) // 2
    room = jnp.where((donor == order[0]) | (receiver == order[0]) | (lengths[receiver] == 0), 0, jnp.maximum(room, 0))
    moved = jax.random.randint(jax.random.fold_in(own, 4), (amount // 2,), 0, 1 << 20) % (room + 1)
    lengths = lengths.at[donor].add(-moved).at[receiver].add(moved)
    members = jnp.searchsorted(jnp.cumsum(lengths), jnp.arange(rows * top), side="right").astype(jnp.int32)
    grid = members.reshape(top, rows).T
    grid = grid[jax.random.permutation(jax.random.fold_in(own, 1), rows)]
    turn = jax.random.randint(jax.random.fold_in(own, 2), (rows, 1), 0, top)
    return jnp.take_along_axis(grid, (jnp.arange(top)[None, :] + turn) % top, axis=1)


def shares(number_of, total, reach, slope, full):
    weights = [(1 << 20) // math.isqrt(grade ** slope) + 1 for grade in range(1, number_of + 1)]
    largest = reach if full else min(reach, max(-(-total // number_of), total * weights[0] // sum(weights)))
    least = 1 if total - largest >= number_of - 1 else 0
    given, surplus = [largest] + [least] * (number_of - 1), total - largest - least * (number_of - 1)
    while surplus > 0:
        candidates = [i for i in range(1, number_of) if given[i] < largest] or [i for i in range(1, number_of) if given[i] < reach]
        whole, budget = sum([weights[i] for i in candidates]), surplus
        for i in candidates:
            extra = min(reach - given[i], max(1, budget * weights[i] // whole), surplus)
            given[i] = given[i] + extra
            surplus = surplus - extra
    return np.array(given)


def scatter_about(stream_key, dims, spread, limit, pieces=(), held_as=jnp.bfloat16):
    values = jax.random.normal(stream_key, dims, jnp.float32) * spread
    if len(pieces) > 0:
        values = shard_levels(stream_key, dims, pieces, -0.22, 0.18) * values
    return jnp.clip(values, min=-limit, max=limit).astype(held_as)


def setup_inputs(seed: int = 0) -> dict:
    key_list = jax.random.split(jax.random.key(seed), 7)
    resid = scatter_about(key_list[0], (ROWS, D), 1.0, 6.0, ((0, 8),))
    enc_weight = scatter_about(key_list[1], (D, F), D ** -0.5, 0.09375, ((1, 32),))
    enc_bias = scatter_about(key_list[2], (F,), 0.5, 3.0, ((0, 32),), jnp.float32)
    dec_weight = scatter_about(key_list[3], (F, D), (ACT * BLK) ** -0.5, 0.0546875, ((0, 32),))
    dec_bias = scatter_about(key_list[4], (D,), 0.5, 3.0, (), jnp.float32)
    active_ids_keys = jax.random.split(jax.random.fold_in(key_list[5], 1), RB // RB)
    active_ids_turns = jax.random.permutation(jax.random.fold_in(key_list[5], 3), RB // RB)
    active_ids = jax.vmap(lambda own, number: shared_out(jax.random.fold_in(key_list[5], 2), own, number, RB, NBLK, ACT, MOST, 2))(active_ids_keys, active_ids_turns).reshape((RB, ACT))
    return dict(resid=resid, enc_weight=enc_weight, enc_bias=enc_bias, dec_weight=dec_weight, dec_bias=dec_bias, active_ids=active_ids)


def reference(resid, enc_weight, enc_bias, dec_weight, dec_bias, active_ids):
    centered = (resid.astype(jnp.float32) - dec_bias[None, :]).astype(jnp.bfloat16)
    enc_blocks = enc_weight.reshape(D, NBLK, BLK)
    dec_blocks = dec_weight.reshape(NBLK, BLK, D)
    bias_blocks = enc_bias.reshape(NBLK, BLK)
    groups = N_TOK * N_FEAT

    def one_rowblock(index):
        rows_here = lax.dynamic_slice_in_dim(centered, index * BLK, BLK, 0)
        ids_here = active_ids[index]
        w_in = jnp.take(enc_blocks, ids_here, axis=1).astype(jnp.float32)
        pre = jnp.einsum("rd,dkh->rkh", rows_here.astype(jnp.float32), w_in)
        pre = pre + jnp.take(bias_blocks, ids_here, axis=0)[None, :, :]
        codes = jnp.maximum(pre, 0.0).astype(jnp.bfloat16)
        w_out = jnp.take(dec_blocks, ids_here, axis=0).astype(jnp.float32)
        contrib = jnp.einsum("rkh,khd->krd", codes.astype(jnp.float32), w_out)
        owners = (ids_here // BLK_DEV).astype(jnp.int32)
        grouped = jax.ops.segment_sum(contrib, owners, num_segments=groups)
        rounded = grouped.astype(jnp.bfloat16).astype(jnp.float32)
        return jnp.sum(rounded, axis=0)

    recon = lax.map(one_rowblock, jnp.arange(RB, dtype=jnp.int32))
    recon = recon.reshape(ROWS, D)
    return recon + dec_bias[None, :] - resid.astype(jnp.float32)
```

```python
import jax
import jax.numpy as jnp
from jax import lax
from jax.experimental import pallas as pl
from jax.experimental.pallas import tpu as pltpu
from jax.sharding import PartitionSpec as P

BLK = 128
BLK_DEV = 8
CHUNKS = 4
MESH = pl.DeviceIdType.MESH


def local(resid, enc_weight, enc_bias, dec_weight, dec_bias, active_ids):
    tok_rows, width = resid.shape
    centered = (resid.astype(jnp.float32) - dec_bias[None, :]).astype(jnp.bfloat16)
    gathered = lax.all_gather(centered, "tok", axis=0, tiled=True)
    row_blocks = gathered.shape[0] // BLK
    tiles = gathered.reshape(row_blocks, BLK, width)
    all_blocks = BLK_DEV * lax.axis_size("tok") * lax.axis_size("feat")
    slot_count = (row_blocks * active_ids.shape[1] + all_blocks - 1) // all_blocks + 1
    device = lax.axis_index("tok") * lax.axis_size("feat") + lax.axis_index("feat")
    owned = device * BLK_DEV + jnp.arange(BLK_DEV, dtype=jnp.int32)
    hits = jnp.any(active_ids[:, :, None] == owned[None, None, :], axis=1)
    ranks = jnp.cumsum(hits.astype(jnp.int32), axis=0) - 1
    slot_range = jnp.arange(slot_count, dtype=jnp.int32)
    match = (hits[:, :, None] & (ranks[:, :, None] == slot_range[None, None, :])).astype(
        jnp.float32
    )
    slot_live = jnp.sum(match, axis=0)

    def one_block(index, partial_value):
        select = lax.dynamic_index_in_dim(match, index, 1, keepdims=False)
        picked = jnp.einsum(
            "rs,rbd->sbd", select.astype(jnp.bfloat16), tiles, preferred_element_type=jnp.float32
        )
        picked = picked.astype(jnp.bfloat16).reshape(slot_count * BLK, width)
        w_in = lax.dynamic_slice_in_dim(enc_weight, index * BLK, BLK, 1)
        bias_in = lax.dynamic_slice_in_dim(enc_bias, index * BLK, BLK, 0)
        pre = jnp.dot(picked, w_in, preferred_element_type=jnp.float32) + bias_in[None, :]
        live = slot_live[index]
        codes = (jnp.maximum(pre, 0.0).reshape(slot_count, BLK, BLK) * live[:, None, None]).astype(
            jnp.bfloat16
        )
        w_out = lax.dynamic_slice_in_dim(dec_weight, index * BLK, BLK, 0)
        contrib = jnp.dot(
            codes.reshape(slot_count * BLK, BLK), w_out, preferred_element_type=jnp.float32
        )
        placed = jnp.einsum(
            "rs,sbd->rbd",
            select,
            contrib.reshape(slot_count, BLK, width),
            precision=lax.Precision.HIGHEST,
        )
        return partial_value + placed

    partial_value = lax.fori_loop(
        0, BLK_DEV, one_block, jnp.zeros((row_blocks, BLK, width), jnp.float32)
    )
    rounded = lax.optimization_barrier(partial_value.astype(jnp.bfloat16)).astype(jnp.float32)
    rounded = rounded.reshape(row_blocks * BLK, width)
    section_one = lax.psum_scatter(
        rounded.astype(jnp.bfloat16), "feat", scatter_dimension=1, tiled=True
    )
    total = lax.psum_scatter(section_one, "tok", scatter_dimension=0, tiled=True).astype(
        jnp.float32
    )
    columns = total.shape[1]
    start = lax.axis_index("feat") * columns
    bias_part = lax.dynamic_slice_in_dim(dec_bias, start, columns, 0)
    resid_part = lax.dynamic_slice_in_dim(resid, start, columns, 1).astype(jnp.float32)
    return total + bias_part[None, :] - resid_part


def fused(resid_ref, enc_ref, ebias_ref, dec_ref, dbias_ref, ids_ref, out_ref,
          xs, enc_v, dec_v, codes, part, from_core, from_first, from_second, from_z, active,
          load_sem, ag_send, ag_recv, core_send, core_recv, first_send, first_recv,
          second_send, second_recv, z_send, z_recv):
    t = lax.axis_index("tok")
    z = lax.axis_index("feat")
    n_z = lax.axis_size("feat")
    core = lax.rem(t, 2)
    chip = t // 2
    x = lax.rem(chip, 2)
    y = chip // 2
    chips = 4
    mine, other = core * chips, (1 - core) * chips
    chip_x, chip_y, chip_d = y * 2 + 1 - x, (1 - y) * 2 + x, (1 - y) * 2 + 1 - x
    sibling = (chip * 2 + 1 - core, z)
    by_x = (chip_x * 2 + core, z)
    by_y = (chip_y * 2 + core, z)
    along_z = [(t, lax.rem(z + d, n_z)) for d in range(1, n_z)]
    width = resid_ref.shape[1]
    own = width // n_z
    step = own // CHUNKS
    half = BLK // 2

    load_enc = pltpu.make_async_copy(enc_ref, enc_v, load_sem.at[0])
    load_dec = pltpu.make_async_copy(dec_ref, dec_v, load_sem.at[1])
    load_enc.start()
    load_dec.start()

    barrier = pltpu.get_barrier_semaphore()
    greeted = [sibling, by_x, by_y] + along_z
    for who in greeted:
        pl.semaphore_signal(barrier, inc=1, device_id=who, device_id_type=MESH)

    def center(i, carry):
        rows = pl.ds(pl.multiple_of(i * 16, 16), 16)
        xs[mine + chip, rows, :] = (
            resid_ref[rows, :].astype(jnp.float32) - dbias_ref[...]
        ).astype(jnp.bfloat16)
        return carry

    lax.fori_loop(0, BLK // 16, center, 0)
    pl.semaphore_wait(barrier, len(greeted))

    sent = []

    def push(src, dst, send, recv, who):
        copy = pltpu.make_async_remote_copy(
            src_ref=src, dst_ref=dst, send_sem=send, recv_sem=recv,
            device_id=who, device_id_type=MESH,
        )
        copy.start()
        sent.append(copy)
        return copy

    def share(n, slot, part_of, who):
        where = xs.at[slot] if part_of is None else xs.at[slot, pl.ds(part_of * half, half), :]
        return push(where, where, ag_send.at[n], ag_recv.at[n], who)

    here = mine + chip
    a1 = share(1, here, 0, by_x)
    a3 = share(3, here, 1, by_y)
    a2 = share(2, here, 1, by_x)
    a4 = share(4, here, 0, by_y)
    a0 = share(0, here, None, sibling)

    ids = ids_ref[...]
    first_block = (t * n_z + z) * BLK_DEV
    for b in range(BLK_DEV):
        hit = jnp.max(jnp.where(ids == first_block + b, 1.0, 0.0), axis=1, keepdims=True)
        active[:, b * BLK:(b + 1) * BLK] = jnp.broadcast_to(hit, (hit.shape[0], BLK))

    def encode(group, chip_of):
        slot = group + chip_of
        row_block = chip_of * 2 + group // chips

        def tile(n, carry):
            cols = pl.ds(pl.multiple_of(n * 256, 256), 256)
            pre = jnp.dot(xs[slot], enc_v[:, cols], preferred_element_type=jnp.float32)
            pre = jnp.maximum(pre + ebias_ref[:, cols], 0.0)
            on = active[pl.ds(row_block, 1), cols]
            codes[slot, :, cols] = jnp.where(on > 0.0, pre, 0.0).astype(jnp.bfloat16)
            return carry

        lax.fori_loop(0, enc_v.shape[1] // 256, tile, 0)

    load_enc.wait()
    encode(mine, chip)
    a0.wait_recv()
    encode(other, chip)
    a1.wait_recv()
    a5 = share(5, mine + chip_x, 0, by_y)
    a3.wait_recv()
    a6 = share(6, mine + chip_y, 1, by_x)
    a2.wait_recv()
    a7 = share(7, mine + chip_x, None, sibling)
    a4.wait_recv()
    a8 = share(8, mine + chip_y, None, sibling)
    encode(mine, chip_x)
    encode(mine, chip_y)
    a7.wait_recv()
    encode(other, chip_x)
    a8.wait_recv()
    encode(other, chip_y)
    a5.wait_recv()
    a9 = share(9, mine + chip_d, 0, sibling)
    a6.wait_recv()
    a10 = share(10, mine + chip_d, 1, sibling)
    load_dec.wait()
    encode(mine, chip_d)
    a9.wait_recv()
    a10.wait_recv()
    encode(other, chip_d)

    def decode(k, group):
        def tile(n, carry):
            cols = pl.ds(pl.multiple_of(n * own + k * step, step), step)
            value = jnp.dot(
                codes[pl.ds(group, chips)].reshape(chips * BLK, codes.shape[2]),
                dec_v[:, cols], preferred_element_type=jnp.float32,
            )
            to = pl.ds(pl.multiple_of(n * step, step), step)
            part[k, pl.ds(group, chips), :, to] = value.astype(jnp.bfloat16).reshape(
                chips, BLK, step
            )
            return carry

        lax.fori_loop(0, n_z, tile, 0)

    def add(k, slot, more):
        part[k, slot] = (
            part[k, slot].astype(jnp.float32) + more.astype(jnp.float32)
        ).astype(jnp.bfloat16)

    def places(k):
        if k % 2 == 0:
            return x, y, by_x, by_y, lambda a, b: b * 2 + a
        return y, x, by_y, by_x, lambda a, b: a * 2 + b

    core_copy, first_copy, second_copy, z_copy = {}, {}, {}, {}

    def make(k):
        decode(k, other)
        core_copy[k] = push(
            part.at[k, pl.ds(other, chips)], from_core.at[k],
            core_send.at[k], core_recv.at[k], sibling,
        )
        decode(k, mine)

    def over_core(k):
        a, b, by_a, by_b, at = places(k)
        core_copy[k].wait_recv()
        for i in range(2):
            away = at(1 - a, i)
            add(k, mine + away, from_core[k, away])
            first_copy[k, i] = push(
                part.at[k, mine + away], from_first.at[k, i],
                first_send.at[k, i], first_recv.at[k, i], by_a,
            )
        for i in range(2):
            kept = at(a, i)
            add(k, mine + kept, from_core[k, kept])

    def over_first(k):
        a, b, by_a, by_b, at = places(k)
        for i in range(2):
            first_copy[k, i].wait_recv()
        add(k, mine + at(a, 1 - b), from_first[k, 1 - b])
        second_copy[k] = push(
            part.at[k, mine + at(a, 1 - b)], from_second.at[k],
            second_send.at[k], second_recv.at[k], by_b,
        )
        add(k, mine + chip, from_first[k, b])

    def over_second(k):
        second_copy[k].wait_recv()
        add(k, mine + chip, from_second[k])
        for d in range(1, n_z):
            cols = pl.ds(pl.multiple_of(along_z[d - 1][1] * step, step), step)
            z_copy[k, d] = push(
                part.at[k, mine + chip, :, cols], from_z.at[k, d - 1],
                z_send.at[k, d - 1], z_recv.at[k, d - 1], along_z[d - 1],
            )

    def over_z(k):
        for d in range(1, n_z):
            z_copy[k, d].wait_recv()
        cols = pl.ds(pl.multiple_of(z * step, step), step)
        total = part[k, mine + chip, :, cols].astype(jnp.float32)
        for d in range(1, n_z):
            total = total + from_z[k, d - 1].astype(jnp.float32)
        there = pl.ds(pl.multiple_of(z * own + k * step, step), step)
        out_ref[:, k * step:(k + 1) * step] = (
            total + dbias_ref[:, there] - resid_ref[:, there].astype(jnp.float32)
        )

    for k in range(CHUNKS):
        make(k)
        if k >= 1:
            over_core(k - 1)
    over_core(CHUNKS - 1)
    for k in range(CHUNKS):
        over_first(k)
        if k >= 1:
            over_second(k - 1)
    over_second(CHUNKS - 1)
    for k in range(CHUNKS):
        over_z(k)
    for copy in sent:
        copy.wait_send()


def fused_local(resid, enc_weight, enc_bias, dec_weight, dec_bias, active_ids):
    n_t, n_z = lax.axis_size("tok"), lax.axis_size("feat")
    rows, width = resid.shape
    feats = enc_weight.shape[1]
    own = width // n_z
    step = own // CHUNKS
    chips = n_t // 2
    vmem = pl.BlockSpec(memory_space=pltpu.VMEM)
    hbm = pl.BlockSpec(memory_space=pl.ANY)
    dma = pltpu.SemaphoreType.DMA
    wide = n_z * step
    return pl.pallas_call(
        fused,
        out_shape=jax.ShapeDtypeStruct((rows, own), jnp.float32),
        in_specs=[vmem, hbm, vmem, hbm, vmem, vmem],
        out_specs=vmem,
        scratch_shapes=[
            pltpu.VMEM((n_t, BLK, width), jnp.bfloat16),
            pltpu.VMEM((width, feats), jnp.bfloat16),
            pltpu.VMEM((feats, width), jnp.bfloat16),
            pltpu.VMEM((n_t, BLK, feats), jnp.bfloat16),
            pltpu.VMEM((CHUNKS, n_t, BLK, wide), jnp.bfloat16),
            pltpu.VMEM((CHUNKS, chips, BLK, wide), jnp.bfloat16),
            pltpu.VMEM((CHUNKS, 2, BLK, wide), jnp.bfloat16),
            pltpu.VMEM((CHUNKS, BLK, wide), jnp.bfloat16),
            pltpu.VMEM((CHUNKS, n_z - 1, BLK, step), jnp.bfloat16),
            pltpu.VMEM((n_t, feats), jnp.float32),
            dma((2,)), dma((11,)), dma((11,)),
            dma((CHUNKS,)), dma((CHUNKS,)), dma((CHUNKS, 2)), dma((CHUNKS, 2)),
            dma((CHUNKS,)), dma((CHUNKS,)), dma((CHUNKS, n_z - 1)), dma((CHUNKS, n_z - 1)),
        ],
        compiler_params=pltpu.CompilerParams(
            collective_id=1, has_side_effects=True, vmem_limit_bytes=60 * 1024 * 1024
        ),
        cost_estimate=pl.CostEstimate(
            flops=4 * n_t * BLK * feats * width, bytes_accessed=4 * feats * width,
            transcendentals=0,
        ),
    )(resid, enc_weight, enc_bias[None, :], dec_weight, dec_bias[None, :], active_ids)


def solution(mesh):
    in_specs = (
        P("tok", None),
        P(None, ("tok", "feat")),
        P(("tok", "feat")),
        P(("tok", "feat"), None),
        P(),
        P(),
    )
    out_specs = P("tok", "feat")
    body = fused_local if mesh.shape["tok"] == 8 else local
    return jax.shard_map(body, mesh=mesh, in_specs=in_specs, out_specs=out_specs, check_vma=False)
```

```python
import jax
import jax.numpy as jnp
from jax import lax
from jax.experimental import pallas as pl
from jax.experimental.pallas import tpu as pltpu
from jax.sharding import PartitionSpec as P

BLK = 128
BLK_DEV = 8
CHUNKS = 8
LEFT = 48
WIDE = BLK - LEFT
MESH = pl.DeviceIdType.MESH


def local(resid, enc_weight, enc_bias, dec_weight, dec_bias, active_ids):
    tok_rows, width = resid.shape
    centered = (resid.astype(jnp.float32) - dec_bias[None, :]).astype(jnp.bfloat16)
    gathered = lax.all_gather(centered, "tok", axis=0, tiled=True)
    row_blocks = gathered.shape[0] // BLK
    tiles = gathered.reshape(row_blocks, BLK, width)
    all_blocks = BLK_DEV * lax.axis_size("tok") * lax.axis_size("feat")
    slot_count = (row_blocks * active_ids.shape[1] + all_blocks - 1) // all_blocks + 1
    device = lax.axis_index("tok") * lax.axis_size("feat") + lax.axis_index("feat")
    owned = device * BLK_DEV + jnp.arange(BLK_DEV, dtype=jnp.int32)
    hits = jnp.any(active_ids[:, :, None] == owned[None, None, :], axis=1)
    ranks = jnp.cumsum(hits.astype(jnp.int32), axis=0) - 1
    slot_range = jnp.arange(slot_count, dtype=jnp.int32)
    match = (hits[:, :, None] & (ranks[:, :, None] == slot_range[None, None, :])).astype(
        jnp.float32
    )
    slot_live = jnp.sum(match, axis=0)

    def one_block(index, partial_value):
        select = lax.dynamic_index_in_dim(match, index, 1, keepdims=False)
        picked = jnp.einsum(
            "rs,rbd->sbd", select.astype(jnp.bfloat16), tiles, preferred_element_type=jnp.float32
        )
        picked = picked.astype(jnp.bfloat16).reshape(slot_count * BLK, width)
        w_in = lax.dynamic_slice_in_dim(enc_weight, index * BLK, BLK, 1)
        bias_in = lax.dynamic_slice_in_dim(enc_bias, index * BLK, BLK, 0)
        pre = jnp.dot(picked, w_in, preferred_element_type=jnp.float32) + bias_in[None, :]
        live = slot_live[index]
        codes = (jnp.maximum(pre, 0.0).reshape(slot_count, BLK, BLK) * live[:, None, None]).astype(
            jnp.bfloat16
        )
        w_out = lax.dynamic_slice_in_dim(dec_weight, index * BLK, BLK, 0)
        contrib = jnp.dot(
            codes.reshape(slot_count * BLK, BLK), w_out, preferred_element_type=jnp.float32
        )
        placed = jnp.einsum(
            "rs,sbd->rbd",
            select,
            contrib.reshape(slot_count, BLK, width),
            precision=lax.Precision.HIGHEST,
        )
        return partial_value + placed

    partial_value = lax.fori_loop(
        0, BLK_DEV, one_block, jnp.zeros((row_blocks, BLK, width), jnp.float32)
    )
    rounded = lax.optimization_barrier(partial_value.astype(jnp.bfloat16)).astype(jnp.float32)
    rounded = rounded.reshape(row_blocks * BLK, width)
    section_one = lax.psum_scatter(
        rounded.astype(jnp.bfloat16), "feat", scatter_dimension=1, tiled=True
    )
    total = lax.psum_scatter(section_one, "tok", scatter_dimension=0, tiled=True).astype(
        jnp.float32
    )
    columns = total.shape[1]
    start = lax.axis_index("feat") * columns
    bias_part = lax.dynamic_slice_in_dim(dec_bias, start, columns, 0)
    resid_part = lax.dynamic_slice_in_dim(resid, start, columns, 1).astype(jnp.float32)
    return total + bias_part[None, :] - resid_part


def fused(resid_ref, enc_ref, ebias_ref, dec_ref, dbias_ref, ids_ref, out_ref,
          xs, late, enc_v, dec_v, codes, part, from_core, from_first, from_second, from_z, active,
          load_sem, ag_send, ag_recv, core_send, core_recv, first_send, first_recv,
          second_send, second_recv, z_send, z_recv):
    t = lax.axis_index("tok")
    z = lax.axis_index("feat")
    n_z = lax.axis_size("feat")
    core = lax.rem(t, 2)
    chip = t // 2
    x = lax.rem(chip, 2)
    y = chip // 2
    chips = 4
    mine, other = core * chips, (1 - core) * chips
    chip_x, chip_y, chip_d = y * 2 + 1 - x, (1 - y) * 2 + x, (1 - y) * 2 + 1 - x
    sibling = (chip * 2 + 1 - core, z)
    by_x = (chip_x * 2 + core, z)
    by_y = (chip_y * 2 + core, z)
    along_z = [(t, lax.rem(z + d, n_z)) for d in range(1, n_z)]
    width = resid_ref.shape[1]
    own = width // n_z
    step = own // CHUNKS
    half = BLK // 2

    load_enc = pltpu.make_async_copy(enc_ref, enc_v, load_sem.at[0])
    load_dec = pltpu.make_async_copy(dec_ref, dec_v, load_sem.at[1])
    load_enc.start()
    load_dec.start()

    barrier = pltpu.get_barrier_semaphore()
    greeted = [sibling, by_x, by_y] + along_z
    for who in greeted:
        pl.semaphore_signal(barrier, inc=1, device_id=who, device_id_type=MESH)

    def center(i, carry):
        rows = pl.ds(pl.multiple_of(i * 16, 16), 16)
        xs[mine + chip, rows, :] = (
            resid_ref[rows, :].astype(jnp.float32) - dbias_ref[...]
        ).astype(jnp.bfloat16)
        return carry

    lax.fori_loop(0, BLK // 16, center, 0)
    pl.semaphore_wait(barrier, len(greeted))

    sent = []

    def push(src, dst, send, recv, who):
        copy = pltpu.make_async_remote_copy(
            src_ref=src, dst_ref=dst, send_sem=send, recv_sem=recv,
            device_id=who, device_id_type=MESH,
        )
        copy.start()
        sent.append(copy)
        return copy

    def share(n, src, dst, who):
        return push(src, dst, ag_send.at[n], ag_recv.at[n], who)

    def rows_of(slot, start, count):
        return xs.at[slot, pl.ds(pl.multiple_of(start, 16), count), :]

    def late_rows(start, count):
        return late.at[core, pl.ds(pl.multiple_of(start, 16), count), :]

    qx = lax.rem(z, 2)
    qy = 1 - qx
    beside = (t, z + 1 - 2 * qx)
    here = mine + chip
    end = BLK - LEFT

    def start_row(n, q, who):
        where = rows_of(here, q * end, LEFT)
        return share(n, where, where, who)

    def middle(n, who):
        where = rows_of(here, LEFT, BLK - 2 * LEFT)
        return share(n, where, where, who)

    a1 = start_row(1, qx, by_x)
    a3 = start_row(3, qy, by_y)
    a2 = middle(2, by_x)
    a4 = middle(4, by_y)
    a0 = share(0, xs.at[here], xs.at[here], sibling)

    ids = ids_ref[...]
    first_block = (t * n_z + z) * BLK_DEV
    for b in range(BLK_DEV):
        hit = jnp.max(jnp.where(ids == first_block + b, 1.0, 0.0), axis=1, keepdims=True)
        active[:, b * BLK:(b + 1) * BLK] = jnp.broadcast_to(hit, (hit.shape[0], BLK))

    def encode(rows, takes):
        def tile(n, carry):
            cols = pl.ds(pl.multiple_of(n * 256, 256), 256)
            pre = jnp.dot(rows[...], enc_v[:, cols], preferred_element_type=jnp.float32)
            pre = jnp.maximum(pre + ebias_ref[:, cols], 0.0)
            for group, chip_of, to, at, count in takes:
                on = active[pl.ds(chip_of * 2 + group // chips, 1), cols]
                codes[group + chip_of, pl.ds(to, count), cols] = jnp.where(
                    on > 0.0, pre[at:at + count], 0.0
                ).astype(jnp.bfloat16)
            return carry

        lax.fori_loop(0, enc_v.shape[1] // 256, tile, 0)

    def encode_wide(group, chip_of, q):
        first = pl.multiple_of(q * LEFT, 16)
        encode(rows_of(group + chip_of, first, WIDE), [(group, chip_of, first, 0, WIDE)])

    def encode_late(group):
        encode(late.at[group // chips], [
            (group, chip_x, pl.multiple_of((1 - qx) * end, 16), 0, LEFT),
            (group, chip_y, pl.multiple_of((1 - qy) * end, 16), LEFT, LEFT),
            (group, chip_d, 0, 2 * LEFT, BLK),
        ])

    load_enc.wait()
    encode(xs.at[here], [(mine, chip, 0, 0, BLK)])
    a1.wait_recv()
    a5 = share(5, rows_of(mine + chip_x, qx * end, LEFT), late_rows(0, LEFT), beside)
    a3.wait_recv()
    a6 = share(6, rows_of(mine + chip_y, qy * end, LEFT), late_rows(LEFT, LEFT), beside)
    a2.wait_recv()
    a7 = share(7, rows_of(mine + chip_x, qx * half, half), late_rows(2 * LEFT + qx * half, half), by_y)
    wide_x = rows_of(mine + chip_x, qx * LEFT, WIDE)
    a9 = share(9, wide_x, wide_x, sibling)
    a4.wait_recv()
    a8 = share(8, rows_of(mine + chip_y, qy * half, half), late_rows(2 * LEFT + qy * half, half), by_x)
    wide_y = rows_of(mine + chip_y, qy * LEFT, WIDE)
    a10 = share(10, wide_y, wide_y, sibling)
    a0.wait_recv()
    encode(xs.at[other + chip], [(other, chip, 0, 0, BLK)])
    encode_wide(mine, chip_x, qx)
    encode_wide(mine, chip_y, qy)
    a9.wait_recv()
    encode_wide(other, chip_x, qx)
    a10.wait_recv()
    encode_wide(other, chip_y, qy)
    a5.wait_recv()
    a11 = share(11, late_rows(0, LEFT), late_rows(0, LEFT), sibling)
    a6.wait_recv()
    a12 = share(12, late_rows(LEFT, LEFT), late_rows(LEFT, LEFT), sibling)
    a7.wait_recv()
    where = late_rows(2 * LEFT + qx * half, half)
    a13 = share(13, where, where, sibling)
    a8.wait_recv()
    where = late_rows(2 * LEFT + qy * half, half)
    a14 = share(14, where, where, sibling)
    encode_late(mine)
    load_dec.wait()
    a11.wait_recv()
    a12.wait_recv()
    a13.wait_recv()
    a14.wait_recv()
    encode_late(other)

    def decode(k, group):
        def tile(n, carry):
            cols = pl.ds(pl.multiple_of(n * own + k * step, 2 * step), 2 * step)
            value = jnp.dot(
                codes[pl.ds(group, chips)].reshape(chips * BLK, codes.shape[2]),
                dec_v[:, cols], preferred_element_type=jnp.float32,
            ).astype(jnp.bfloat16).reshape(chips, BLK, 2 * step)
            to = pl.ds(pl.multiple_of(n * step, step), step)
            part[k, pl.ds(group, chips), :, to] = value[:, :, :step]
            part[k + 1, pl.ds(group, chips), :, to] = value[:, :, step:]
            return carry

        lax.fori_loop(0, n_z, tile, 0)

    def add(k, slot, more):
        part[k, slot] = (
            part[k, slot].astype(jnp.float32) + more.astype(jnp.float32)
        ).astype(jnp.bfloat16)

    def places(k):
        if k % 2 == 0:
            return x, y, by_x, by_y, lambda a, b: b * 2 + a
        return y, x, by_y, by_x, lambda a, b: a * 2 + b

    core_copy, first_copy, second_copy, z_copy = {}, {}, {}, {}

    def make(j):
        decode(2 * j, other)
        for k in (2 * j, 2 * j + 1):
            core_copy[k] = push(
                part.at[k, pl.ds(other, chips)], from_core.at[k],
                core_send.at[k], core_recv.at[k], sibling,
            )
        decode(2 * j, mine)

    def over_core(k):
        a, b, by_a, by_b, at = places(k)
        core_copy[k].wait_recv()
        for i in range(2):
            away = at(1 - a, i)
            add(k, mine + away, from_core[k, away])
            first_copy[k, i] = push(
                part.at[k, mine + away], from_first.at[k, i],
                first_send.at[k, i], first_recv.at[k, i], by_a,
            )
        for i in range(2):
            kept = at(a, i)
            add(k, mine + kept, from_core[k, kept])

    def over_first(k):
        a, b, by_a, by_b, at = places(k)
        for i in range(2):
            first_copy[k, i].wait_recv()
        add(k, mine + at(a, 1 - b), from_first[k, 1 - b])
        second_copy[k] = push(
            part.at[k, mine + at(a, 1 - b)], from_second.at[k],
            second_send.at[k], second_recv.at[k], by_b,
        )
        add(k, mine + chip, from_first[k, b])

    def over_second(k):
        second_copy[k].wait_recv()
        add(k, mine + chip, from_second[k])
        for d in range(1, n_z):
            cols = pl.ds(pl.multiple_of(along_z[d - 1][1] * step, step), step)
            z_copy[k, d] = push(
                part.at[k, mine + chip, :, cols], from_z.at[k, d - 1],
                z_send.at[k, d - 1], z_recv.at[k, d - 1], along_z[d - 1],
            )

    def over_z(k):
        for d in range(1, n_z):
            z_copy[k, d].wait_recv()
        cols = pl.ds(pl.multiple_of(z * step, step), step)
        total = part[k, mine + chip, :, cols].astype(jnp.float32)
        for d in range(1, n_z):
            total = total + from_z[k, d - 1].astype(jnp.float32)
        there = pl.ds(pl.multiple_of(z * own + k * step, step), step)
        out_ref[:, k * step:(k + 1) * step] = (
            total + dbias_ref[:, there] - resid_ref[:, there].astype(jnp.float32)
        )

    def both(stage, j):
        if 0 <= j < pairs:
            stage(2 * j)
            stage(2 * j + 1)

    pairs = CHUNKS // 2
    make(0)
    make(1)
    both(over_core, 0)
    for j in range(2, pairs):
        make(j)
        both(over_core, j - 1) if j == 2 else None
    for j in range(pairs):
        both(over_first, j)
        both(over_core, j + 2)
        both(over_second, j - 1)
    both(over_second, pairs - 1)
    for k in range(CHUNKS):
        over_z(k)
    for copy in sent:
        copy.wait_send()


def fused_local(resid, enc_weight, enc_bias, dec_weight, dec_bias, active_ids):
    n_t, n_z = lax.axis_size("tok"), lax.axis_size("feat")
    rows, width = resid.shape
    feats = enc_weight.shape[1]
    own = width // n_z
    step = own // CHUNKS
    chips = n_t // 2
    vmem = pl.BlockSpec(memory_space=pltpu.VMEM)
    hbm = pl.BlockSpec(memory_space=pl.ANY)
    dma = pltpu.SemaphoreType.DMA
    wide = n_z * step
    return pl.pallas_call(
        fused,
        out_shape=jax.ShapeDtypeStruct((rows, own), jnp.float32),
        in_specs=[vmem, hbm, vmem, hbm, vmem, vmem],
        out_specs=vmem,
        scratch_shapes=[
            pltpu.VMEM((n_t, BLK, width), jnp.bfloat16),
            pltpu.VMEM((2, 2 * LEFT + BLK, width), jnp.bfloat16),
            pltpu.VMEM((width, feats), jnp.bfloat16),
            pltpu.VMEM((feats, width), jnp.bfloat16),
            pltpu.VMEM((n_t, BLK, feats), jnp.bfloat16),
            pltpu.VMEM((CHUNKS, n_t, BLK, wide), jnp.bfloat16),
            pltpu.VMEM((CHUNKS, chips, BLK, wide), jnp.bfloat16),
            pltpu.VMEM((CHUNKS, 2, BLK, wide), jnp.bfloat16),
            pltpu.VMEM((CHUNKS, BLK, wide), jnp.bfloat16),
            pltpu.VMEM((CHUNKS, n_z - 1, BLK, step), jnp.bfloat16),
            pltpu.VMEM((n_t, feats), jnp.float32),
            dma((2,)), dma((15,)), dma((15,)),
            dma((CHUNKS,)), dma((CHUNKS,)), dma((CHUNKS, 2)), dma((CHUNKS, 2)),
            dma((CHUNKS,)), dma((CHUNKS,)), dma((CHUNKS, n_z - 1)), dma((CHUNKS, n_z - 1)),
        ],
        compiler_params=pltpu.CompilerParams(
            collective_id=1, has_side_effects=True, vmem_limit_bytes=60 * 1024 * 1024
        ),
        cost_estimate=pl.CostEstimate(
            flops=4 * n_t * BLK * feats * width, bytes_accessed=4 * feats * width,
            transcendentals=0,
        ),
    )(resid, enc_weight, enc_bias[None, :], dec_weight, dec_bias[None, :], active_ids)


def solution(mesh):
    in_specs = (
        P("tok", None),
        P(None, ("tok", "feat")),
        P(("tok", "feat")),
        P(("tok", "feat"), None),
        P(),
        P(),
    )
    out_specs = P("tok", "feat")
    body = fused_local if mesh.shape["tok"] == 8 else local
    return jax.shard_map(body, mesh=mesh, in_specs=in_specs, out_specs=out_specs, check_vma=False)
```

```python
import jax
import jax.numpy as jnp
from jax import lax
from jax.experimental import pallas as pl
from jax.experimental.pallas import tpu as pltpu
from jax.sharding import PartitionSpec as P

BLK = 128
BLK_DEV = 8
CHUNKS = 8
LEFT = 48
WIDE = BLK - LEFT
MESH = pl.DeviceIdType.MESH


def local(resid, enc_weight, enc_bias, dec_weight, dec_bias, active_ids):
    tok_rows, width = resid.shape
    centered = (resid.astype(jnp.float32) - dec_bias[None, :]).astype(jnp.bfloat16)
    gathered = lax.all_gather(centered, "tok", axis=0, tiled=True)
    row_blocks = gathered.shape[0] // BLK
    tiles = gathered.reshape(row_blocks, BLK, width)
    all_blocks = BLK_DEV * lax.axis_size("tok") * lax.axis_size("feat")
    slot_count = (row_blocks * active_ids.shape[1] + all_blocks - 1) // all_blocks + 1
    device = lax.axis_index("tok") * lax.axis_size("feat") + lax.axis_index("feat")
    owned = device * BLK_DEV + jnp.arange(BLK_DEV, dtype=jnp.int32)
    hits = jnp.any(active_ids[:, :, None] == owned[None, None, :], axis=1)
    ranks = jnp.cumsum(hits.astype(jnp.int32), axis=0) - 1
    slot_range = jnp.arange(slot_count, dtype=jnp.int32)
    match = (hits[:, :, None] & (ranks[:, :, None] == slot_range[None, None, :])).astype(
        jnp.float32
    )
    slot_live = jnp.sum(match, axis=0)

    def one_block(index, partial_value):
        select = lax.dynamic_index_in_dim(match, index, 1, keepdims=False)
        picked = jnp.einsum(
            "rs,rbd->sbd", select.astype(jnp.bfloat16), tiles, preferred_element_type=jnp.float32
        )
        picked = picked.astype(jnp.bfloat16).reshape(slot_count * BLK, width)
        w_in = lax.dynamic_slice_in_dim(enc_weight, index * BLK, BLK, 1)
        bias_in = lax.dynamic_slice_in_dim(enc_bias, index * BLK, BLK, 0)
        pre = jnp.dot(picked, w_in, preferred_element_type=jnp.float32) + bias_in[None, :]
        live = slot_live[index]
        codes = (jnp.maximum(pre, 0.0).reshape(slot_count, BLK, BLK) * live[:, None, None]).astype(
            jnp.bfloat16
        )
        w_out = lax.dynamic_slice_in_dim(dec_weight, index * BLK, BLK, 0)
        contrib = jnp.dot(
            codes.reshape(slot_count * BLK, BLK), w_out, preferred_element_type=jnp.float32
        )
        placed = jnp.einsum(
            "rs,sbd->rbd",
            select,
            contrib.reshape(slot_count, BLK, width),
            precision=lax.Precision.HIGHEST,
        )
        return partial_value + placed

    partial_value = lax.fori_loop(
        0, BLK_DEV, one_block, jnp.zeros((row_blocks, BLK, width), jnp.float32)
    )
    rounded = lax.optimization_barrier(partial_value.astype(jnp.bfloat16)).astype(jnp.float32)
    rounded = rounded.reshape(row_blocks * BLK, width)
    section_one = lax.psum_scatter(
        rounded.astype(jnp.bfloat16), "feat", scatter_dimension=1, tiled=True
    )
    total = lax.psum_scatter(section_one, "tok", scatter_dimension=0, tiled=True).astype(
        jnp.float32
    )
    columns = total.shape[1]
    start = lax.axis_index("feat") * columns
    bias_part = lax.dynamic_slice_in_dim(dec_bias, start, columns, 0)
    resid_part = lax.dynamic_slice_in_dim(resid, start, columns, 1).astype(jnp.float32)
    return total + bias_part[None, :] - resid_part


def fused(resid_ref, enc_ref, ebias_ref, dec_ref, dbias_ref, ids_ref, out_ref,
          xs, late, enc_v, dec_v, codes, part, from_core, from_first, from_second, from_z, active,
          load_sem, ag_send, ag_recv, core_send, core_recv, first_send, first_recv,
          second_send, second_recv, z_send, z_recv):
    t = lax.axis_index("tok")
    z = lax.axis_index("feat")
    n_z = lax.axis_size("feat")
    core = lax.rem(t, 2)
    chip = t // 2
    x = lax.rem(chip, 2)
    y = chip // 2
    chips = 4
    mine, other = core * chips, (1 - core) * chips
    chip_x, chip_y, chip_d = y * 2 + 1 - x, (1 - y) * 2 + x, (1 - y) * 2 + 1 - x
    sibling = (chip * 2 + 1 - core, z)
    by_x = (chip_x * 2 + core, z)
    by_y = (chip_y * 2 + core, z)
    along_z = [(t, lax.rem(z + d, n_z)) for d in range(1, n_z)]
    width = resid_ref.shape[1]
    own = width // n_z
    step = own // CHUNKS
    half = BLK // 2

    load_enc = pltpu.make_async_copy(enc_ref, enc_v, load_sem.at[0])
    load_dec = pltpu.make_async_copy(dec_ref, dec_v, load_sem.at[1])
    load_enc.start()
    load_dec.start()

    barrier = pltpu.get_barrier_semaphore()
    greeted = [sibling, by_x, by_y] + along_z
    for who in greeted:
        pl.semaphore_signal(barrier, inc=1, device_id=who, device_id_type=MESH)

    def center(i, carry):
        rows = pl.ds(pl.multiple_of(i * 16, 16), 16)
        xs[mine + chip, rows, :] = (
            resid_ref[rows, :].astype(jnp.float32) - dbias_ref[...]
        ).astype(jnp.bfloat16)
        return carry

    lax.fori_loop(0, BLK // 16, center, 0)
    pl.semaphore_wait(barrier, len(greeted))

    sent = []

    def push(src, dst, send, recv, who):
        copy = pltpu.make_async_remote_copy(
            src_ref=src, dst_ref=dst, send_sem=send, recv_sem=recv,
            device_id=who, device_id_type=MESH,
        )
        copy.start()
        sent.append(copy)
        return copy

    def share(n, src, dst, who):
        return push(src, dst, ag_send.at[n], ag_recv.at[n], who)

    def rows_of(slot, start, count):
        return xs.at[slot, pl.ds(pl.multiple_of(start, 16), count), :]

    def late_rows(start, count):
        return late.at[core, pl.ds(pl.multiple_of(start, 16), count), :]

    qx = lax.rem(z, 2)
    qy = 1 - qx
    beside = (t, z + 1 - 2 * qx)
    here = mine + chip
    end = BLK - LEFT

    def start_row(n, q, who):
        where = rows_of(here, q * end, LEFT)
        return share(n, where, where, who)

    def middle(n, who):
        where = rows_of(here, LEFT, BLK - 2 * LEFT)
        return share(n, where, where, who)

    a1 = start_row(1, qx, by_x)
    a3 = start_row(3, qy, by_y)
    a2 = middle(2, by_x)
    a4 = middle(4, by_y)
    a0 = share(0, xs.at[here], xs.at[here], sibling)

    ids = ids_ref[...]
    first_block = (t * n_z + z) * BLK_DEV
    for b in range(BLK_DEV):
        hit = jnp.max(jnp.where(ids == first_block + b, 1.0, 0.0), axis=1, keepdims=True)
        active[:, b * BLK:(b + 1) * BLK] = jnp.broadcast_to(hit, (hit.shape[0], BLK))

    def encode(rows, takes):
        def tile(n, carry):
            cols = pl.ds(pl.multiple_of(n * 256, 256), 256)
            pre = jnp.dot(rows[...], enc_v[:, cols], preferred_element_type=jnp.float32)
            pre = jnp.maximum(pre + ebias_ref[:, cols], 0.0)
            for group, chip_of, to, at, count in takes:
                on = active[pl.ds(chip_of * 2 + group // chips, 1), cols]
                codes[group + chip_of, pl.ds(to, count), cols] = jnp.where(
                    on > 0.0, pre[at:at + count], 0.0
                ).astype(jnp.bfloat16)
            return carry

        lax.fori_loop(0, enc_v.shape[1] // 256, tile, 0)

    def encode_wide(group, chip_of, q):
        first = pl.multiple_of(q * LEFT, 16)
        encode(rows_of(group + chip_of, first, WIDE), [(group, chip_of, first, 0, WIDE)])

    def encode_late(group):
        encode(late.at[group // chips], [
            (group, chip_x, pl.multiple_of((1 - qx) * end, 16), 0, LEFT),
            (group, chip_y, pl.multiple_of((1 - qy) * end, 16), LEFT, LEFT),
            (group, chip_d, 0, 2 * LEFT, BLK),
        ])

    load_enc.wait()
    encode(xs.at[here], [(mine, chip, 0, 0, BLK)])
    a1.wait_recv()
    a5 = share(5, rows_of(mine + chip_x, qx * end, LEFT), late_rows(0, LEFT), beside)
    a3.wait_recv()
    a6 = share(6, rows_of(mine + chip_y, qy * end, LEFT), late_rows(LEFT, LEFT), beside)
    a2.wait_recv()
    a7 = share(7, rows_of(mine + chip_x, qx * half, half), late_rows(2 * LEFT + qx * half, half), by_y)
    wide_x = rows_of(mine + chip_x, qx * LEFT, WIDE)
    a9 = share(9, wide_x, wide_x, sibling)
    a4.wait_recv()
    a8 = share(8, rows_of(mine + chip_y, qy * half, half), late_rows(2 * LEFT + qy * half, half), by_x)
    wide_y = rows_of(mine + chip_y, qy * LEFT, WIDE)
    a10 = share(10, wide_y, wide_y, sibling)
    a0.wait_recv()
    encode(xs.at[other + chip], [(other, chip, 0, 0, BLK)])
    encode_wide(mine, chip_x, qx)
    encode_wide(mine, chip_y, qy)
    a9.wait_recv()
    encode_wide(other, chip_x, qx)
    a10.wait_recv()
    encode_wide(other, chip_y, qy)
    a5.wait_recv()
    a11 = share(11, late_rows(0, LEFT), late_rows(0, LEFT), sibling)
    a6.wait_recv()
    a12 = share(12, late_rows(LEFT, LEFT), late_rows(LEFT, LEFT), sibling)
    a7.wait_recv()
    where = late_rows(2 * LEFT + qx * half, half)
    a13 = share(13, where, where, sibling)
    a8.wait_recv()
    where = late_rows(2 * LEFT + qy * half, half)
    a14 = share(14, where, where, sibling)
    encode_late(mine)
    load_dec.wait()
    a11.wait_recv()
    a12.wait_recv()
    a13.wait_recv()
    a14.wait_recv()
    encode_late(other)

    def decode(k, group):
        def tile(n, carry):
            cols = pl.ds(pl.multiple_of(n * own + k * step, 2 * step), 2 * step)
            value = jnp.dot(
                codes[pl.ds(group, chips)].reshape(chips * BLK, codes.shape[2]),
                dec_v[:, cols], preferred_element_type=jnp.float32,
            ).astype(jnp.bfloat16).reshape(chips, BLK, 2 * step)
            to = pl.ds(pl.multiple_of(n * step, step), step)
            part[k, pl.ds(group, chips), :, to] = value[:, :, :step]
            part[k + 1, pl.ds(group, chips), :, to] = value[:, :, step:]
            return carry

        lax.fori_loop(0, n_z, tile, 0)

    def add(k, slot, more):
        part[k, slot] = (
            part[k, slot].astype(jnp.float32) + more.astype(jnp.float32)
        ).astype(jnp.bfloat16)

    def places(k):
        if k % 2 == 0:
            return x, y, by_x, by_y, lambda a, b: b * 2 + a
        return y, x, by_y, by_x, lambda a, b: a * 2 + b

    core_copy, first_copy, second_copy, z_copy = {}, {}, {}, {}

    def make(j):
        decode(2 * j, other)
        for k in (2 * j, 2 * j + 1):
            core_copy[k] = push(
                part.at[k, pl.ds(other, chips)], from_core.at[k],
                core_send.at[k], core_recv.at[k], sibling,
            )
        decode(2 * j, mine)

    def over_core(k):
        a, b, by_a, by_b, at = places(k)
        core_copy[k].wait_recv()
        for i in range(2):
            away = at(1 - a, i)
            add(k, mine + away, from_core[k, away])
            first_copy[k, i] = push(
                part.at[k, mine + away], from_first.at[k, i],
                first_send.at[k, i], first_recv.at[k, i], by_a,
            )
        for i in range(2):
            kept = at(a, i)
            add(k, mine + kept, from_core[k, kept])

    def over_first(k):
        a, b, by_a, by_b, at = places(k)
        for i in range(2):
            first_copy[k, i].wait_recv()
        add(k, mine + at(a, 1 - b), from_first[k, 1 - b])
        second_copy[k] = push(
            part.at[k, mine + at(a, 1 - b)], from_second.at[k],
            second_send.at[k], second_recv.at[k], by_b,
        )
        add(k, mine + chip, from_first[k, b])

    def over_second(k):
        second_copy[k].wait_recv()
        add(k, mine + chip, from_second[k])
        for d in range(1, n_z):
            cols = pl.ds(pl.multiple_of(along_z[d - 1][1] * step, step), step)
            z_copy[k, d] = push(
                part.at[k, mine + chip, :, cols], from_z.at[k, d - 1],
                z_send.at[k, d - 1], z_recv.at[k, d - 1], along_z[d - 1],
            )

    def over_z(k):
        for d in range(1, n_z):
            z_copy[k, d].wait_recv()
        cols = pl.ds(pl.multiple_of(z * step, step), step)
        total = part[k, mine + chip, :, cols].astype(jnp.float32)
        for d in range(1, n_z):
            total = total + from_z[k, d - 1].astype(jnp.float32)
        there = pl.ds(pl.multiple_of(z * own + k * step, step), step)
        out_ref[:, k * step:(k + 1) * step] = (
            total + dbias_ref[:, there] - resid_ref[:, there].astype(jnp.float32)
        )

    def both(stage, j):
        if 0 <= j < pairs:
            stage(2 * j)
            stage(2 * j + 1)

    pairs = CHUNKS // 2
    make(0)
    both(over_core, 0)
    make(1)
    both(over_core, 1)
    make(2)
    both(over_first, 0)
    both(over_core, 2)
    for j in range(3, pairs):
        make(j)
    for j in range(1, pairs):
        both(over_first, j)
        both(over_core, j + 2)
        both(over_second, j - 1)
        both(over_z, j - 2)
    both(over_second, pairs - 1)
    both(over_z, pairs - 2)
    both(over_z, pairs - 1)
    for copy in sent:
        copy.wait_send()


def fused_local(resid, enc_weight, enc_bias, dec_weight, dec_bias, active_ids):
    n_t, n_z = lax.axis_size("tok"), lax.axis_size("feat")
    rows, width = resid.shape
    feats = enc_weight.shape[1]
    own = width // n_z
    step = own // CHUNKS
    chips = n_t // 2
    vmem = pl.BlockSpec(memory_space=pltpu.VMEM)
    hbm = pl.BlockSpec(memory_space=pl.ANY)
    dma = pltpu.SemaphoreType.DMA
    wide = n_z * step
    return pl.pallas_call(
        fused,
        out_shape=jax.ShapeDtypeStruct((rows, own), jnp.float32),
        in_specs=[vmem, hbm, vmem, hbm, vmem, vmem],
        out_specs=vmem,
        scratch_shapes=[
            pltpu.VMEM((n_t, BLK, width), jnp.bfloat16),
            pltpu.VMEM((2, 2 * LEFT + BLK, width), jnp.bfloat16),
            pltpu.VMEM((width, feats), jnp.bfloat16),
            pltpu.VMEM((feats, width), jnp.bfloat16),
            pltpu.VMEM((n_t, BLK, feats), jnp.bfloat16),
            pltpu.VMEM((CHUNKS, n_t, BLK, wide), jnp.bfloat16),
            pltpu.VMEM((CHUNKS, chips, BLK, wide), jnp.bfloat16),
            pltpu.VMEM((CHUNKS, 2, BLK, wide), jnp.bfloat16),
            pltpu.VMEM((CHUNKS, BLK, wide), jnp.bfloat16),
            pltpu.VMEM((CHUNKS, n_z - 1, BLK, step), jnp.bfloat16),
            pltpu.VMEM((n_t, feats), jnp.float32),
            dma((2,)), dma((15,)), dma((15,)),
            dma((CHUNKS,)), dma((CHUNKS,)), dma((CHUNKS, 2)), dma((CHUNKS, 2)),
            dma((CHUNKS,)), dma((CHUNKS,)), dma((CHUNKS, n_z - 1)), dma((CHUNKS, n_z - 1)),
        ],
        compiler_params=pltpu.CompilerParams(
            collective_id=1, has_side_effects=True, vmem_limit_bytes=60 * 1024 * 1024
        ),
        cost_estimate=pl.CostEstimate(
            flops=4 * n_t * BLK * feats * width, bytes_accessed=4 * feats * width,
            transcendentals=0,
        ),
    )(resid, enc_weight, enc_bias[None, :], dec_weight, dec_bias[None, :], active_ids)


def solution(mesh):
    in_specs = (
        P("tok", None),
        P(None, ("tok", "feat")),
        P(("tok", "feat")),
        P(("tok", "feat"), None),
        P(),
        P(),
    )
    out_specs = P("tok", "feat")
    body = fused_local if mesh.shape["tok"] == 8 else local
    return jax.shard_map(body, mesh=mesh, in_specs=in_specs, out_specs=out_specs, check_vma=False)
```
